256 devices in a mesh: tenant: 8 (over z), replica: 4 (over x), row: 8 (over y, core).
Axes of the slice: x: 4, y: 4, z: 8, core: 2. Of those that a mesh axis runs over, the one named last changes fastest.
Arguments:
- acts: bfloat16 [8192, 8192], P('row', 'replica'), may hold values from -6 to 6
- base_weight: bfloat16 [8192, 8192], P('replica', 'tenant'), may hold values from -0.0625 to 0.0625
- delta_blocks: bfloat16 [16, 208, 128, 128], P('tenant', 'replica'), may hold values from -0.25 to 0.25
- block_index: int32 [16, 208], P('tenant', 'replica'), may hold values from 0 to 1023, as said below
- tenant_counts: int32 [8, 16], P('row'), may hold values from 1 to 256, as said below
Outputs:
- projected: bfloat16 [8192, 8192], P('row', ('tenant', 'replica'))
The draws below stay inside these ranges and needn't reach their ends.
Inputs may be any that keep to these rules, and one draw needn't show every extreme that they name: Each row of tenant_counts sums to 1024; exactly one entry of each row equals 256, and at least one equals 1. `block_index`: the 52 entries of one tenant and one quarter (entries q * 52 to (q + 1) * 52 - 1) are distinct.
All inputs are finite; a program needn't handle non-finite values.
Results may differ from the reference program's by a relative error of at most 0.015.
Values may be sent and summed in bfloat16 or wider, within the bound.
A program may use at most 192 MiB of HBM per device.

```python
import jax
import jax.numpy as jnp
from jax import lax

D = 8192
NBR = 52
R_DEV = 1024
CAP = 256
TENANTS = 16
NB = 208
GROUPS = 8
ROWS = 8192
NBC = 64
BQ = 16


def draw_tenant_counts(key, part):
    keys = jax.random.split(key, GROUPS)
    others = TENANTS - 1
    rest = R_DEV - CAP
    base = rest // others
    remain = rest - base * others
    pairs = others // 2

    def one_group(group_key):
        first, second = jax.random.split(group_key, 2)
        order = jax.random.permutation(first, TENANTS)
        shifts = jax.random.randint(second, (pairs,), 0, max(base, 1)).astype(jnp.int32)
        shifts = shifts.at[0].set(base - 1)
        values = jnp.full((others,), base, jnp.int32)
        values = values.at[0:2 * pairs:2].add(-shifts).at[1:2 * pairs:2].add(shifts)
        values = values + (jnp.arange(others) >= others - remain).astype(jnp.int32)
        ordered = jnp.concatenate([jnp.full((1,), CAP, jnp.int32), values])
        return jnp.zeros((TENANTS,), jnp.int32).at[order].set(ordered)
    return jax.vmap(one_group)(keys)


def draw_block_index(key, part):
    quarters = NB // NBR
    keys = jax.random.split(jax.random.fold_in(key, 7), TENANTS * quarters)

    def one_list(list_key):
        chosen = jax.random.permutation(list_key, BQ * NBC)[:NBR]
        return jnp.sort(chosen).astype(jnp.int32)
    return jax.vmap(one_list)(keys).reshape(TENANTS, NB)


def shard_levels(key, extent, cuts, low, high):
    gain = 1.0
    for position, blocks in cuts:
        heights = jax.random.uniform(jax.random.fold_in(jax.random.fold_in(key, 6), position), (blocks,), jnp.float32, low / len(cuts), high / len(cuts))
        gain = gain * jnp.repeat(jnp.exp(heights), extent[position] // blocks).reshape((-1,) + (1,) * (len(extent) - 1 - position))
    return gain


def scatter_about(key, dims, scale, limit, pieces=(), held_as=jnp.bfloat16):
    loudness = shard_levels(key, dims, pieces, -0.22, 0.18) if pieces else 1.0
    array = jax.random.normal(key, dims, jnp.float32) * scale * loudness
    return jnp.minimum(jnp.maximum(array, -limit), limit).astype(held_as)


def setup_inputs(seed: int = 0) -> dict:
    key_list = jax.random.split(jax.random.key(seed), 6)
    acts = scatter_about(key_list[0], (ROWS, D), 1.0, 6.0, ((0, 8), (1, 4)))
    base_weight = scatter_about(key_list[1], (D, D), D ** -0.5, 0.0625, ((0, 4), (1, 8)))
    delta_blocks = scatter_about(key_list[2], (TENANTS, NB, 128, 128), 512 ** -0.5, 0.25, ((0, 8), (1, 4)))
    block_index = draw_block_index(jax.random.fold_in(key_list[5], 71), 0)
    tenant_counts = draw_tenant_counts(jax.random.fold_in(key_list[5], 71), 0)
    return dict(acts=acts, base_weight=base_weight, delta_blocks=delta_blocks, block_index=block_index, tenant_counts=tenant_counts)


def reference(acts, base_weight, delta_blocks, block_index, tenant_counts):
    rows_all, width = acts.shape
    nbc = width // 128
    quarters = NB // NBR
    bq = nbc // quarters
    base = jnp.dot(acts, base_weight, preferred_element_type=jnp.float32)
    offsets = (jnp.cumsum(tenant_counts, axis=1) - tenant_counts).astype(jnp.int32)
    slots = jnp.arange(CAP).astype(jnp.int32)
    group_start = (jnp.arange(GROUPS) * R_DEV).astype(jnp.int32)
    quarter_of = (jnp.arange(NB) // NBR).astype(jnp.int32)

    def per_tenant(t, total):
        start = offsets[:, t]
        count = tenant_counts[:, t]
        local = start[:, None] + slots[None, :]
        rowid = (group_start[:, None] + jnp.minimum(local, R_DEV - 1)).reshape(-1).astype(jnp.int32)
        valid = (slots[None, :] < count[:, None]).reshape(-1)
        target = jnp.where(valid, (group_start[:, None] + local).reshape(-1), rows_all).astype(jnp.int32)
        picked = jnp.take(acts, rowid, axis=0)
        pos = block_index[t]
        brow = (quarter_of * bq + pos // nbc).astype(jnp.int32)
        bcol = (pos % nbc).astype(jnp.int32)
        tiles = picked.reshape(-1, nbc, 128)
        chosen = jnp.take(tiles, brow, axis=1).astype(jnp.float32)
        contrib = jnp.einsum('mnk,nkl->nml', chosen, delta_blocks[t].astype(jnp.float32),
                             precision=lax.Precision.HIGHEST)
        segment = (quarter_of * nbc + bcol).astype(jnp.int32)
        summed = jax.ops.segment_sum(contrib, segment, num_segments=quarters * nbc)
        share = jnp.transpose(summed.reshape(quarters, nbc, -1, 128), (2, 0, 1, 3)).reshape(-1, quarters, width)
        share = jnp.where(valid[:, None, None], share, 0.0)
        share = lax.optimization_barrier(share.astype(jnp.bfloat16)).astype(jnp.float32)
        delta = jnp.sum(share, axis=1)
        return total.at[target].add(delta, mode="drop")

    total = lax.fori_loop(0, TENANTS, per_tenant, jnp.zeros((rows_all, width), jnp.float32))
    return (base + total).astype(jnp.bfloat16)
```

```python
import functools

import jax
import jax.numpy as jnp
from jax import lax
from jax.experimental import pallas as pl
from jax.experimental.pallas import tpu as pltpu
from jax.sharding import PartitionSpec as P

SLOTS = 28
COUNT = 127
OFFSETS = (1, 7, 2, 6, 3, 5, 4)
MESH = pl.DeviceIdType.MESH
MIB = 1 << 20


def pack_kernel(round_ref, index_ref, delta_ref, send_ref, lists_ref, slab, sem):
    part = lax.axis_index("row")
    load = pltpu.make_async_copy(
        delta_ref.at[:, pl.ds(pl.multiple_of(part * 16, 16), 16), :], slab, sem
    )
    load.start()
    first = round_ref[0] * SLOTS
    for dest in range(8):
        lists_ref[dest, COUNT] = 0
    load.wait()
    tenants, tiles = index_ref.shape
    for tenant in range(tenants):

        def place(n, carry):
            where = index_ref[tenant, n]
            dest = lax.shift_right_logical(where & 63, 3)
            count = lists_ref[dest, COUNT]
            tile = tenant * tiles + n
            lists_ref[dest, count] = where + tenant * 1024 + tile * 2048
            lists_ref[dest, COUNT] = count + 1
            slot = count - first
            slot = jnp.where((slot >= 0) & (slot < SLOTS), slot, SLOTS)
            send_ref[dest, slot] = slab[tile]
            return carry

        lax.fori_loop(0, tiles, place, 0)


def pack(step, block_index, delta):
    return pl.pallas_call(
        pack_kernel,
        out_shape=(
            jax.ShapeDtypeStruct((8, SLOTS + 1, 16, 128), jnp.bfloat16),
            jax.ShapeDtypeStruct((8, 128), jnp.int32),
        ),
        in_specs=[
            pl.BlockSpec(memory_space=pltpu.SMEM),
            pl.BlockSpec(memory_space=pltpu.SMEM),
            pl.BlockSpec(memory_space=pl.ANY),
        ],
        out_specs=(
            pl.BlockSpec(memory_space=pltpu.VMEM),
            pl.BlockSpec(memory_space=pltpu.SMEM),
        ),
        scratch_shapes=[
            pltpu.VMEM((delta.shape[0], 16, 128), jnp.bfloat16),
            pltpu.SemaphoreType.DMA,
        ],
        name="pack_tiles",
    )(step, block_index, delta)


def exchange_kernel(with_base, *refs):
    if with_base:
        send, lists, acts, weight, recv, all_lists, base = refs[:7]
        rest = refs[7:]
        acts_v, weight_v, base_v, load_sem, store_sem = rest[-5:]
    else:
        send, lists, recv, all_lists = refs[:4]
        rest = refs[4:]
    (z_s, z_r, l_s, l_r, own_sem, up_s, up_r, dn_s, dn_r, fu_s, fu_r, fd_s, fd_r, co_s, co_r) = rest[:15]
    t = lax.axis_index("tenant")
    part = lax.axis_index("row")
    core = part % 2
    y = part // 2
    up = ((y + 1) % 4) * 2 + core
    down = ((y + 3) % 4) * 2 + core
    far = ((y + 2) % 4) * 2 + core
    twin = y * 2 + (1 - core)
    half = SLOTS // 2

    if with_base:
        loads = [
            pltpu.make_async_copy(weight, weight_v, load_sem.at[0]),
            pltpu.make_async_copy(acts, acts_v, load_sem.at[1]),
        ]
        for load in loads:
            load.start()
    own = pltpu.make_async_copy(lists, all_lists.at[t], own_sem)
    own.start()

    barrier = pltpu.get_barrier_semaphore()
    for k in OFFSETS:
        pl.semaphore_signal(barrier, inc=1, device_id={"tenant": (t + k) % 8}, device_id_type=MESH)
    for other in (up, down, twin):
        pl.semaphore_signal(barrier, inc=1, device_id={"row": other}, device_id_type=MESH)
    pl.semaphore_wait(barrier, 10)

    def remote(src, dst, s, r, who):
        return pltpu.make_async_remote_copy(
            src_ref=src, dst_ref=dst, send_sem=s, recv_sem=r, device_id=who, device_id_type=MESH
        )

    z_copies = []
    for i, k in enumerate(OFFSETS):
        dest = (t + k) % 8
        copy = remote(
            send.at[dest, pl.ds(0, SLOTS)], recv.at[t, part], z_s.at[i], z_r.at[i], {"tenant": dest}
        )
        copy.start()
        z_copies.append(copy)
    for i, k in enumerate(OFFSETS):
        copy = remote(lists, all_lists.at[t], l_s.at[i], l_r.at[i], {"tenant": (t + k) % 8})
        copy.start()
        z_copies.append(copy)

    sent = []
    up_c, dn_c, fu_c, fd_c, co_c = {}, {}, {}, {}, {}

    def go(copy):
        copy.start()
        sent.append(copy)
        return copy

    for i in range(9):
        if i < 7:
            src = (t - OFFSETS[i] + 8) % 8
            z_copies[i].wait_recv()
            block = recv.at[src, part]
            up_c[i] = go(remote(block, block, up_s.at[i], up_r.at[i], {"row": up}))
            dn_c[i] = go(remote(block, block, dn_s.at[i], dn_r.at[i], {"row": down}))
            co_c[i, 0] = go(remote(block, block, co_s.at[i, 0], co_r.at[i, 0], {"row": twin}))
        j = i - 1
        if 0 <= j < 7:
            src = (t - OFFSETS[j] + 8) % 8
            up_c[j].wait_recv()
            block = recv.at[src, down]
            piece = recv.at[src, down, pl.ds(0, half)]
            fu_c[j] = go(remote(piece, piece, fu_s.at[j], fu_r.at[j], {"row": up}))
            co_c[j, 1] = go(remote(block, block, co_s.at[j, 1], co_r.at[j, 1], {"row": twin}))
            dn_c[j].wait_recv()
            block = recv.at[src, up]
            piece = recv.at[src, up, pl.ds(half, SLOTS - half)]
            fd_c[j] = go(remote(piece, piece, fd_s.at[j], fd_r.at[j], {"row": down}))
            co_c[j, 2] = go(remote(block, block, co_s.at[j, 2], co_r.at[j, 2], {"row": twin}))
        j = i - 2
        if 0 <= j < 7:
            src = (t - OFFSETS[j] + 8) % 8
            fu_c[j].wait_recv()
            fd_c[j].wait_recv()
            block = recv.at[src, far]
            co_c[j, 3] = go(remote(block, block, co_s.at[j, 3], co_r.at[j, 3], {"row": twin}))
        if with_base and i < 4:
            if i == 0:
                for load in loads:
                    load.wait()
            rows = pl.ds(i * 256, 256)

            @pl.loop(0, 4)
            def _(c):
                out = jnp.dot(
                    acts_v[rows, :],
                    weight_v[:, pl.ds(pl.multiple_of(c * 256, 256), 256)],
                    preferred_element_type=jnp.float32,
                )
                base_v[2 * c, rows, :] = out[:, :128]
                base_v[2 * c + 1, rows, :] = out[:, 128:]

            if i == 3:
                store = pltpu.make_async_copy(base_v, base, store_sem)
                store.start()
    for i in range(7):
        for n in range(4):
            co_c[i, n].wait_recv()
    for i in range(7, 14):
        z_copies[i].wait_recv()
    for copy in z_copies + sent:
        copy.wait_send()
    own.wait()
    if with_base:
        store.wait()


def exchange(send, lists, acts=None, weight=None):
    with_base = acts is not None
    sems = [pltpu.SemaphoreType.DMA((7,))] * 4 + [pltpu.SemaphoreType.DMA]
    sems += [pltpu.SemaphoreType.DMA((7,))] * 8 + [pltpu.SemaphoreType.DMA((7, 4))] * 2
    out_shape = [
        jax.ShapeDtypeStruct((8, 8, SLOTS, 16, 128), jnp.bfloat16),
        jax.ShapeDtypeStruct((8, 8, 128), jnp.int32),
    ]
    operands = [send, lists]
    if with_base:
        rows, depth = acts.shape
        columns = weight.shape[1]
        operands += [acts, weight]
        out_shape.append(jax.ShapeDtypeStruct((columns // 128, rows, 128), jnp.float32))
        sems += [
            pltpu.VMEM((rows, depth), jnp.bfloat16),
            pltpu.VMEM((depth, columns), jnp.bfloat16),
            pltpu.VMEM((columns // 128, rows, 128), jnp.float32),
            pltpu.SemaphoreType.DMA((2,)),
            pltpu.SemaphoreType.DMA,
        ]
    return pl.pallas_call(
        functools.partial(exchange_kernel, with_base),
        out_shape=tuple(out_shape),
        in_specs=[pl.BlockSpec(memory_space=pl.ANY)] * len(operands),
        out_specs=tuple([pl.BlockSpec(memory_space=pl.ANY)] * len(out_shape)),
        scratch_shapes=sems,
        compiler_params=pltpu.CompilerParams(
            collective_id=0 if with_base else 1,
            has_side_effects=True,
            vmem_limit_bytes=(24 if with_base else 4) * MIB,
        ),
        name="exchange_tiles_base" if with_base else "exchange_tiles",
    )(*operands)


GROUP = 4
CHUNK = 128


def delta_kernel(
    first_round, round_ref, lists_ref, counts_ref, acts, delta, recv, start_ref, out_ref,
    offsets, acts_v, own_v, recv_v, acc, sems,
):
    t = lax.axis_index("tenant")
    low = round_ref[0] * SLOTS
    loads = [pltpu.make_async_copy(acts, acts_v, sems.at[0])]
    if first_round:
        loads.append(pltpu.make_async_copy(start_ref, acc, sems.at[9]))
        loads.append(pltpu.make_async_copy(delta, own_v, sems.at[8]))
    for k in range(1, 8):
        loads.append(pltpu.make_async_copy(recv.at[(t + k) % 8], recv_v.at[k], sems.at[k]))
    for load in loads:
        load.start()
    total = jnp.int32(0)
    for tenant in range(16):
        offsets[tenant] = total
        total = total + counts_ref[0, tenant]
    rows = acts_v.shape[0]
    if not first_round:
        for d in range(4):
            acc[2 * d] = start_ref[d, :, :128].astype(jnp.float32)
            acc[2 * d + 1] = start_ref[d, :, 128:].astype(jnp.float32)

    line = lax.broadcasted_iota(jnp.int32, (CHUNK, 128), 0)

    def apply(src, count, begin, tile_of):
        def group(g, carry):
            work = []
            chunks = jnp.int32(0)
            for u in range(GROUP):
                j = g * GROUP + u
                valid = j < count
                j = jnp.minimum(j, count - 1)
                entry = lists_ref[src, t, begin + j]
                tenant = 2 * src + (lax.shift_right_logical(entry, 10) & 1)
                brow = lax.shift_right_logical(entry, 6) & 15
                bcol = entry & 7
                lo = offsets[tenant]
                hi = jnp.where(valid, lo + counts_ref[0, tenant], 0)
                base = lax.shift_right_logical(lo, 4) * 16
                chunks = jnp.maximum(chunks, lax.shift_right_arithmetic(hi - base + CHUNK - 1, 7))
                work.append((j, entry, brow, bcol, lo, hi, base))

            def chunk(i, carry):
                products = []
                for j, entry, brow, bcol, lo, hi, base in work:
                    at = pl.multiple_of(jnp.minimum(base + i * CHUNK, rows - CHUNK), 16)
                    x = acts_v[pl.ds(at, CHUNK), pl.ds(pl.multiple_of(brow * 128, 128), 128)]
                    out = jnp.dot(x, tile_of(j, entry), preferred_element_type=jnp.float32)
                    products.append((at, jnp.maximum(lo, base + i * CHUNK), hi, bcol, out))
                for at, lo, hi, bcol, out in products:
                    keep = (line >= lo - at) & (line < hi - at)
                    acc[bcol, pl.ds(at, CHUNK), :] += jnp.where(keep, out, 0.0)
                return carry

            lax.fori_loop(0, chunks, chunk, 0)
            return carry

        lax.fori_loop(0, lax.shift_right_logical(count + GROUP - 1, 2), group, 0)

    for load in loads[: 3 if first_round else 1]:
        load.wait()
    if first_round:
        apply(t, lists_ref[t, t, COUNT], 0, lambda j, entry: own_v[lax.shift_right_logical(entry, 11)])
    for k in range(1, 8):
        src = (t + k) % 8
        loads[(2 if first_round else 0) + k].wait()
        count = jnp.clip(lists_ref[src, t, COUNT] - low, 0, SLOTS)
        apply(src, count, low, lambda j, entry, k=k: recv_v[k, :, j].reshape(128, 128))

    @pl.loop(0, 8)
    def _(i):
        span = pl.ds(pl.multiple_of(i * 128, 128), 128)
        for d in range(4):
            out_ref[d, span, :128] = acc[2 * d, span, :].astype(jnp.bfloat16)
            out_ref[d, span, 128:] = acc[2 * d + 1, span, :].astype(jnp.bfloat16)


def add_delta(step, all_lists, counts, acts, delta, recv, start, first_round):
    rows, depth = acts.shape
    any_spec = pl.BlockSpec(memory_space=pl.ANY)
    smem = pl.BlockSpec(memory_space=pltpu.SMEM)
    vmem = pl.BlockSpec(memory_space=pltpu.VMEM)
    return pl.pallas_call(
        functools.partial(delta_kernel, first_round),
        out_shape=jax.ShapeDtypeStruct((4, rows, 256), jnp.bfloat16),
        in_specs=[smem, smem, smem, any_spec, any_spec, any_spec, any_spec if first_round else vmem],
        out_specs=vmem,
        scratch_shapes=[
            pltpu.SMEM((16,), jnp.int32),
            pltpu.VMEM((rows, depth), jnp.bfloat16),
            pltpu.VMEM(delta.shape, jnp.bfloat16),
            pltpu.VMEM(recv.shape, jnp.bfloat16),
            pltpu.VMEM((8, rows, 128), jnp.float32),
            pltpu.SemaphoreType.DMA((10,)),
        ],
        compiler_params=pltpu.CompilerParams(vmem_limit_bytes=40 * MIB),
        name="add_delta",
    )(step, all_lists, counts, acts, delta, recv, start)


PIECES = 4


def reduce_kernel(
    part, out_ref, mine, in_a, in_b, f_a, f_b, g_a, g_b, s_a, s_b, load_sem, send_sem, recv_sem
):
    me = lax.axis_index("replica")
    right, left, far = (me + 1) % 4, (me + 3) % 4, (me + 2) % 4
    half = part.shape[1] // 2
    size = half // PIECES

    loads = [
        pltpu.make_async_copy(part.at[right, pl.ds(0, half)], mine.at[0], load_sem.at[0]),
        pltpu.make_async_copy(part.at[left, pl.ds(half, half)], mine.at[1], load_sem.at[1]),
        pltpu.make_async_copy(part.at[me, pl.ds(0, half)], mine.at[2], load_sem.at[2]),
        pltpu.make_async_copy(part.at[me, pl.ds(half, half)], mine.at[3], load_sem.at[3]),
    ]
    for load in loads:
        load.start()
    barrier = pltpu.get_barrier_semaphore()
    for who in (right, left):
        pl.semaphore_signal(barrier, inc=1, device_id={"replica": who}, device_id_type=MESH)
    pl.semaphore_wait(barrier, 2)

    started = []

    def send(kind, piece, src, dst, who):
        copy = pltpu.make_async_remote_copy(
            src_ref=src,
            dst_ref=dst,
            send_sem=send_sem.at[kind, piece],
            recv_sem=recv_sem.at[kind, piece],
            device_id={"replica": who},
            device_id_type=MESH,
        )
        copy.start()
        started.append(copy)
        return copy

    ins_a, ins_b, fs_a, fs_b, gs_a, gs_b = [], [], [], [], [], []
    for p in range(PIECES):
        span = pl.ds(p * size, size)
        low, high = pl.ds(p * size, size), pl.ds(half + p * size, size)
        ins_a.append(send(0, p, part.at[far, low], in_a.at[span], right))
        ins_b.append(send(1, p, part.at[far, high], in_b.at[span], left))
    for p in range(PIECES):
        span = pl.ds(p * size, size)
        low, high = pl.ds(p * size, size), pl.ds(half + p * size, size)
        fs_b.append(send(2, p, part.at[right, high], f_b.at[span], right))
        fs_a.append(send(3, p, part.at[left, low], f_a.at[span], left))
    loads[0].wait()
    loads[1].wait()
    for p in range(PIECES):
        span = pl.ds(p * size, size)
        ins_a[p].wait_recv()
        s_a[span, :] = (mine[0, span, :].astype(jnp.float32) + in_a[span, :].astype(jnp.float32)).astype(jnp.bfloat16)
        gs_a.append(send(4, p, s_a.at[span], g_a.at[span], right))
        ins_b[p].wait_recv()
        s_b[span, :] = (mine[1, span, :].astype(jnp.float32) + in_b[span, :].astype(jnp.float32)).astype(jnp.bfloat16)
        gs_b.append(send(5, p, s_b.at[span], g_b.at[span], left))
    loads[2].wait()
    loads[3].wait()
    for p in range(PIECES):
        span = pl.ds(p * size, size)
        fs_a[p].wait_recv()
        gs_a[p].wait_recv()
        out_ref[pl.ds(p * size, size), :] = (
            mine[2, span, :].astype(jnp.float32) + f_a[span, :].astype(jnp.float32) + g_a[span, :].astype(jnp.float32)
        ).astype(jnp.bfloat16)
        fs_b[p].wait_recv()
        gs_b[p].wait_recv()
        out_ref[pl.ds(half + p * size, size), :] = (
            mine[3, span, :].astype(jnp.float32) + f_b[span, :].astype(jnp.float32) + g_b[span, :].astype(jnp.float32)
        ).astype(jnp.bfloat16)
    for copy in started:
        copy.wait_send()


def reduce_blocks(part):
    _, rows, columns = part.shape
    half = rows // 2
    return pl.pallas_call(
        reduce_kernel,
        out_shape=jax.ShapeDtypeStruct((rows, columns), jnp.bfloat16),
        in_specs=[pl.BlockSpec(memory_space=pl.ANY)],
        out_specs=pl.BlockSpec(memory_space=pltpu.VMEM),
        scratch_shapes=[pltpu.VMEM((4, half, columns), jnp.bfloat16)]
        + [pltpu.VMEM((half, columns), jnp.bfloat16)] * 8
        + [
            pltpu.SemaphoreType.DMA((4,)),
            pltpu.SemaphoreType.DMA((6, PIECES)),
            pltpu.SemaphoreType.DMA((6, PIECES)),
        ],
        compiler_params=pltpu.CompilerParams(
            collective_id=2, has_side_effects=True, vmem_limit_bytes=16 * MIB
        ),
        name="reduce_blocks",
    )(part)


def body(acts, base_weight, delta_blocks, block_index, tenant_counts):
    delta = delta_blocks.reshape(-1, 128, 128)
    here = lax.axis_index("tenant")
    step = jnp.zeros((1,), jnp.int32)
    send, lists = pack(step, block_index, delta)
    lengths = jnp.where(jnp.arange(8) == here, 0, lists[:, COUNT])
    longest = lax.pmax(jnp.max(lengths), ("tenant", "replica"))
    recv, all_lists, base = exchange(send, lists, acts, base_weight)
    part = add_delta(step, all_lists, tenant_counts, acts, delta, recv, base, True)

    def another(n, part):
        step = jnp.full((1,), n, jnp.int32)
        send, lists = pack(step, block_index, delta)
        recv, all_lists = exchange(send, lists)
        return add_delta(step, all_lists, tenant_counts, acts, delta, recv, part, False)

    part = lax.fori_loop(1, (longest + SLOTS - 1) // SLOTS, another, part)
    return reduce_blocks(part)


def solution(mesh):
    placed = (
        P("row", "replica"),
        P("replica", "tenant"),
        P("tenant", "replica", None, None),
        P("tenant", "replica"),
        P("row", None),
    )
    return jax.shard_map(
        body, mesh=mesh, in_specs=placed, out_specs=P("row", ("tenant", "replica")), check_vma=False
    )
```

```python
import functools

import jax
import jax.numpy as jnp
from jax import lax
from jax.experimental import pallas as pl
from jax.experimental.pallas import tpu as pltpu
from jax.sharding import PartitionSpec as P

SLOTS = 28
HALF = SLOTS // 2
SPARE = 28
GATHERED = 7 * HALF + SPARE
STARTS = (0, 2 * HALF, 4 * HALF, 6 * HALF, 7 * HALF)
SIZES = (2 * HALF, 2 * HALF, 2 * HALF, HALF, SPARE)
COUNT = 127
AHEAD = 8
OFFSETS = (1, 7, 2, 6, 3, 5, 4)
MESH = pl.DeviceIdType.MESH
MIB = 1 << 20


def list_kernel(index_ref, lists_ref):
    tenants, tiles = index_ref.shape
    counts = (jnp.int32(0), jnp.int32(0))
    for tenant in range(tenants):

        def place(n, counts):
            where = index_ref[tenant, n]
            dest = lax.shift_right_logical(where & 63, 3)
            byte = (dest & 3) * 8
            first = dest < 4
            word = jnp.where(first, counts[0], counts[1])
            count = lax.shift_right_logical(word, byte) & 255
            lists_ref[dest, count] = where + tenant * 1024 + (tenant * tiles + n) * 2048
            one = lax.shift_left(jnp.int32(1), byte)
            return counts[0] + jnp.where(first, one, 0), counts[1] + jnp.where(first, 0, one)

        counts = lax.fori_loop(0, tiles, place, counts, unroll=4)
    for dest in range(8):
        lists_ref[dest, COUNT] = lax.shift_right_logical(counts[dest // 4], (dest % 4) * 8) & 255


def list_tiles(block_index):
    return pl.pallas_call(
        list_kernel,
        out_shape=jax.ShapeDtypeStruct((8, 128), jnp.int32),
        in_specs=[pl.BlockSpec(memory_space=pltpu.SMEM)],
        out_specs=pl.BlockSpec(memory_space=pltpu.SMEM),
        compiler_params=pltpu.CompilerParams(vmem_limit_bytes=1 * MIB),
        cost_estimate=pl.CostEstimate(flops=0, bytes_accessed=8 * MIB, transcendentals=0),
        name="list_tiles",
    )(block_index)


def pick(lists_ref, slab, out_ref, dest, first):
    count = lists_ref[dest, COUNT]

    def one(s, carry):
        at = first + s
        entry = lists_ref[dest, jnp.minimum(at, COUNT)]
        tile = jnp.where(at < count, lax.shift_right_logical(entry, 11), 0)
        out_ref[s] = slab[tile]
        return carry

    lax.fori_loop(0, SLOTS, one, 0, unroll=4)


def send_to(axis):
    def remote(src, dst, s, r, who):
        return pltpu.make_async_remote_copy(
            src_ref=src, dst_ref=dst, send_sem=s, recv_sem=r, device_id={axis: who}, device_id_type=MESH
        )

    return remote


def ring():
    part = lax.axis_index("row")
    core = part % 2
    y = part // 2
    up = ((y + 1) % 4) * 2 + core
    down = ((y + 3) % 4) * 2 + core
    far = ((y + 2) % 4) * 2 + core
    twin = y * 2 + (1 - core)
    return part, up, down, far, twin


def greet(t, up, down, twin):
    barrier = pltpu.get_barrier_semaphore()
    for k in OFFSETS:
        pl.semaphore_signal(barrier, inc=1, device_id={"tenant": (t + k) % 8}, device_id_type=MESH)
    for other in (up, down, twin):
        pl.semaphore_signal(barrier, inc=1, device_id={"row": other}, device_id_type=MESH)
    pl.semaphore_wait(barrier, 10)


def first_exchange_kernel(
    lists_ref, lists, delta, acts, weight, recv, all_lists, base, acts_v,
    slab, outgoing, second, known, weight_v, load_sem,
    z_s, z_r, l_s, l_r, up_s, up_r, dn_s, dn_r, fw_s, fw_r, co_s, co_r,
):
    t = lax.axis_index("tenant")
    part, up, down, far, twin = ring()
    tenant_copy, row_copy = send_to("tenant"), send_to("row")
    loads = [
        pltpu.make_async_copy(
            delta.at[:, pl.ds(pl.multiple_of(part * 16, 16), 16), :], slab, load_sem.at[0]
        ),
        pltpu.make_async_copy(lists, all_lists.at[t], load_sem.at[1]),
        pltpu.make_async_copy(weight, weight_v, load_sem.at[2]),
        pltpu.make_async_copy(acts, acts_v, load_sem.at[3]),
    ]
    for load in loads:
        load.start()
    greet(t, up, down, twin)

    sent = []

    def go(copy):
        copy.start()
        sent.append(copy)
        return copy

    tables = []
    for i, k in enumerate(OFFSETS):
        tables.append(go(tenant_copy(lists, all_lists.at[t], l_s.at[i], l_r.at[i], (t + k) % 8)))
    loads[0].wait()
    z_copies = []
    for i, k in enumerate(OFFSETS):
        dest = (t + k) % 8
        pick(lists_ref, slab, outgoing.at[i], dest, 0)
        copy = tenant_copy(
            outgoing.at[i, pl.ds(0, HALF)], recv.at[part, pl.ds(i * HALF, HALF)], z_s.at[i], z_r.at[i], dest
        )
        if i < AHEAD:
            go(copy)
        z_copies.append(copy)
    for i, k in enumerate(OFFSETS):
        copy = tenant_copy(
            outgoing.at[i, pl.ds(HALF, HALF)], second.at[i], z_s.at[7 + i], z_r.at[7 + i], (t + k) % 8
        )
        if 7 + i < AHEAD:
            go(copy)
        z_copies.append(copy)
    loads[1].wait()
    for table in tables:
        table.wait_recv()
    learn = pltpu.make_async_copy(all_lists, known, load_sem.at[4])
    learn.start()
    learn.wait()

    ups, downs, forwards, twins = {}, {}, {}, []

    def spans(g):
        half = SIZES[g] // 2
        return pl.ds(STARTS[g], half), pl.ds(STARTS[g] + half, half)

    def share(g, n, owner):
        block = recv.at[owner, pl.ds(STARTS[g], SIZES[g])]
        twins.append(go(row_copy(block, block, co_s.at[g, n], co_r.at[g, n], twin)))

    def landed(i):
        z_copies[i].wait_recv()
        if i + AHEAD < 14:
            go(z_copies[i + AHEAD])

    def compact():
        ends = []
        total = jnp.int32(0)
        for k in OFFSETS:
            total = total + jnp.clip(known[(t + 8 - k) % 8, t, COUNT] - HALF, 0, HALF)
            ends.append(total)

        def one(s, carry):
            src, begin = jnp.int32(0), jnp.int32(0)
            for end in ends:
                past = s >= end
                src = src + jnp.where(past, 1, 0)
                begin = jnp.where(past, end, begin)
            recv[part, STARTS[4] + s] = second[jnp.minimum(src, 6), jnp.clip(s - begin, 0, HALF - 1)]
            return carry

        lax.fori_loop(0, SPARE, one, 0, unroll=2)

    def spread(g):
        low, high = spans(g)
        a, b = recv.at[part, low], recv.at[part, high]
        ups[g, 0] = go(row_copy(a, a, up_s.at[g, 0], up_r.at[g, 0], up))
        downs[g, 1] = go(row_copy(b, b, dn_s.at[g, 1], dn_r.at[g, 1], down))
        ups[g, 1] = go(row_copy(b, b, up_s.at[g, 1], up_r.at[g, 1], up))
        downs[g, 0] = go(row_copy(a, a, dn_s.at[g, 0], dn_r.at[g, 0], down))
        share(g, 0, part)

    def neighbours(g):
        low, high = spans(g)
        ups[g, 0].wait_recv()
        a = recv.at[down, low]
        forwards[g, 0] = go(row_copy(a, a, fw_s.at[g, 0], fw_r.at[g, 0], up))
        downs[g, 1].wait_recv()
        b = recv.at[up, high]
        forwards[g, 1] = go(row_copy(b, b, fw_s.at[g, 1], fw_r.at[g, 1], down))
        ups[g, 1].wait_recv()
        share(g, 1, down)
        downs[g, 0].wait_recv()
        share(g, 2, up)

    def opposite(g):
        forwards[g, 0].wait_recv()
        forwards[g, 1].wait_recv()
        share(g, 3, far)

    def multiply(i):
        if i == 0:
            loads[2].wait()
            loads[3].wait()
        rows = pl.ds(i * 256, 256)

        @pl.loop(0, 4)
        def _(c):
            out = jnp.dot(
                acts_v[rows, :],
                weight_v[:, pl.ds(pl.multiple_of(c * 256, 256), 256)],
                preferred_element_type=jnp.float32,
            )
            base[2 * c, rows, :] = out[:, :128]
            base[2 * c + 1, rows, :] = out[:, 128:]

    def arrived(g):
        for i in (2 * g, 2 * g + 1) if g < 3 else (6,):
            landed(i)
        spread(g)

    arrived(0)
    multiply(0)
    arrived(1)
    neighbours(0)
    multiply(1)
    arrived(2)
    opposite(0)
    neighbours(1)
    multiply(2)
    arrived(3)
    neighbours(2)
    opposite(1)
    landed(7)
    landed(8)
    multiply(3)
    neighbours(3)
    opposite(2)
    landed(9)
    landed(10)
    opposite(3)
    landed(11)
    landed(12)
    landed(13)
    compact()
    spread(4)
    neighbours(4)
    opposite(4)
    for copy in twins:
        copy.wait_recv()
    for copy in sent:
        copy.wait_send()


def first_exchange(lists, delta, acts, weight):
    rows, depth = acts.shape
    columns = weight.shape[1]
    any_spec = pl.BlockSpec(memory_space=pl.ANY)
    vmem = pl.BlockSpec(memory_space=pltpu.VMEM)
    dma = pltpu.SemaphoreType.DMA
    return pl.pallas_call(
        first_exchange_kernel,
        out_shape=(
            jax.ShapeDtypeStruct((8, GATHERED, 16, 128), jnp.bfloat16),
            jax.ShapeDtypeStruct((8, 8, 128), jnp.int32),
            jax.ShapeDtypeStruct((columns // 128, rows, 128), jnp.float32),
            jax.ShapeDtypeStruct((rows, depth), jnp.bfloat16),
        ),
        in_specs=[
            pl.BlockSpec(memory_space=pltpu.SMEM),
            any_spec,
            any_spec,
            pl.BlockSpec(memory_space=pltpu.HBM),
            pl.BlockSpec(memory_space=pltpu.HBM),
        ],
        out_specs=(vmem, any_spec, vmem, vmem),
        scratch_shapes=[
            pltpu.VMEM((delta.shape[0], 16, 128), jnp.bfloat16),
            pltpu.VMEM((7, SLOTS, 16, 128), jnp.bfloat16),
        ]
        + [
            pltpu.VMEM((7, HALF, 16, 128), jnp.bfloat16),
            pltpu.SMEM((8, 8, 128), jnp.int32),
            pltpu.VMEM((depth, columns), jnp.bfloat16),
            dma((5,)),
        ]
        + [dma((14,))] * 2
        + [dma((7,))] * 2
        + [dma((5, 2))] * 6
        + [dma((5, 4))] * 2,
        compiler_params=pltpu.CompilerParams(
            collective_id=0, has_side_effects=True, vmem_limit_bytes=28 * MIB
        ),
        name="exchange_tiles_base",
    )(lists, lists, delta, acts, weight)


def exchange_kernel(
    round_ref, lists_ref, delta, unused_weight, recv, slab, outgoing, load_sem,
    z_s, z_r, up_s, up_r, dn_s, dn_r, fw_s, fw_r, co_s, co_r,
):
    t = lax.axis_index("tenant")
    part, up, down, far, twin = ring()
    tenant_copy, row_copy = send_to("tenant"), send_to("row")
    load = pltpu.make_async_copy(
        delta.at[:, pl.ds(pl.multiple_of(part * 16, 16), 16), :], slab, load_sem
    )
    load.start()
    greet(t, up, down, twin)
    load.wait()
    half = SLOTS // 2
    low, high = pl.ds(0, half), pl.ds(half, half)
    for i, k in enumerate(OFFSETS):
        dest = (t + k) % 8
        src = (t + 8 - k) % 8
        pick(lists_ref, slab, outgoing.at[i], dest, round_ref[0] * SLOTS)
        copies = [tenant_copy(outgoing.at[i], recv.at[t, part], z_s.at[i], z_r.at[i], dest)]
        copies[0].start()
        copies[0].wait_recv()

        def go(block, s, r, who):
            copy = row_copy(block, block, s, r, who)
            copy.start()
            copies.append(copy)
            return copy

        block = recv.at[src, part]
        raised = go(block, up_s.at[i], up_r.at[i], up)
        lowered = go(block, dn_s.at[i], dn_r.at[i], down)
        twins = [go(block, co_s.at[i, 0], co_r.at[i, 0], twin)]
        raised.wait_recv()
        lowered.wait_recv()
        one = go(recv.at[src, down, low], fw_s.at[i, 0], fw_r.at[i, 0], up)
        two = go(recv.at[src, up, high], fw_s.at[i, 1], fw_r.at[i, 1], down)
        twins.append(go(recv.at[src, down], co_s.at[i, 1], co_r.at[i, 1], twin))
        twins.append(go(recv.at[src, up], co_s.at[i, 2], co_r.at[i, 2], twin))
        one.wait_recv()
        two.wait_recv()
        twins.append(go(recv.at[src, far], co_s.at[i, 3], co_r.at[i, 3], twin))
        for copy in twins:
            copy.wait_recv()
        for copy in copies:
            copy.wait_send()


def exchange(step, lists, delta, weight):
    dma = pltpu.SemaphoreType.DMA
    return pl.pallas_call(
        exchange_kernel,
        out_shape=jax.ShapeDtypeStruct((8, 8, SLOTS, 16, 128), jnp.bfloat16),
        in_specs=[pl.BlockSpec(memory_space=pltpu.SMEM)] * 2 + [pl.BlockSpec(memory_space=pl.ANY)] * 2,
        out_specs=pl.BlockSpec(memory_space=pltpu.VMEM),
        scratch_shapes=[
            pltpu.VMEM((delta.shape[0], 16, 128), jnp.bfloat16),
            pltpu.VMEM((7, SLOTS, 16, 128), jnp.bfloat16),
            dma,
        ]
        + [dma((7,))] * 6
        + [dma((7, 2))] * 2
        + [dma((7, 4))] * 2,
        compiler_params=pltpu.CompilerParams(
            collective_id=1, has_side_effects=True, vmem_limit_bytes=16 * MIB
        ),
        name="exchange_tiles",
    )(step, lists, delta, weight)


GROUP = 8
CHUNK = 128


def delta_kernel(
    first_round, round_ref, lists_ref, counts_ref, acts_v, own_v, recv, start_ref, out_ref, flag_ref,
    offsets, acc,
):
    t = lax.axis_index("tenant")
    low = round_ref[0] * SLOTS
    rows = acts_v.shape[0]
    longest, over = jnp.int32(0), jnp.int32(0)
    for dest in range(8):
        spare = jnp.int32(0)
        for k in range(1, 8):
            length = lists_ref[(dest + k) % 8, dest, COUNT]
            longest = jnp.maximum(longest, length)
            spare = spare + jnp.maximum(length - HALF, 0)
        over = jnp.maximum(over, spare - SPARE)
    over = jnp.maximum(over, longest - SLOTS)
    flag_ref[...] = jnp.full(flag_ref.shape, jnp.where(over > 0, longest, 0), jnp.int32)
    total = jnp.int32(0)
    for tenant in range(16):
        offsets[tenant] = total
        total = total + counts_ref[0, tenant]
    if first_round:
        acc = start_ref
    else:
        acc[...] = jnp.zeros_like(acc)

    line = lax.broadcasted_iota(jnp.int32, (CHUNK, 128), 0)

    def apply(src, begin, end, tile_of):
        def group(g, carry):
            work = []
            chunks = jnp.int32(0)
            for u in range(GROUP):
                j = begin + g * GROUP + u
                valid = j < end
                j = jnp.minimum(j, end - 1)
                entry = lists_ref[src, t, j]
                tenant = 2 * src + (lax.shift_right_logical(entry, 10) & 1)
                brow = lax.shift_right_logical(entry, 6) & 15
                bcol = entry & 7
                lo = offsets[tenant]
                hi = jnp.where(valid, lo + counts_ref[0, tenant], 0)
                base = lax.shift_right_logical(lo, 4) * 16
                chunks = jnp.maximum(chunks, lax.shift_right_arithmetic(hi - base + CHUNK - 1, 7))
                work.append((j, entry, brow, bcol, lo, hi, base))

            def chunk(i, carry):
                products = []
                for j, entry, brow, bcol, lo, hi, base in work:
                    at = pl.multiple_of(jnp.minimum(base + i * CHUNK, rows - CHUNK), 16)
                    x = acts_v[pl.ds(at, CHUNK), pl.ds(pl.multiple_of(brow * 128, 128), 128)]
                    out = jnp.dot(x, tile_of(j, entry), preferred_element_type=jnp.float32)
                    products.append((at, jnp.maximum(lo, base + i * CHUNK), hi, bcol, out))
                for at, lo, hi, bcol, out in products:
                    keep = (line >= lo - at) & (line < hi - at)
                    acc[bcol, pl.ds(at, CHUNK), :] += jnp.where(keep, out, 0.0)
                return carry

            lax.fori_loop(0, chunks, chunk, 0)
            return carry

        lax.fori_loop(0, lax.div(jnp.maximum(end - begin, 0) + GROUP - 1, GROUP), group, 0)

    begin = jnp.int32(0)
    for i, k in enumerate(OFFSETS):
        src = (t + 8 - k) % 8
        count = lists_ref[src, t, COUNT]
        served = jnp.minimum(count, HALF + jnp.clip(SPARE - begin, 0, HALF))
        later = 7 * HALF + begin - HALF
        begin = begin + jnp.clip(count - HALF, 0, HALF)
        if first_round:
            apply(
                src,
                0,
                served,
                lambda j, entry, i=i, later=later: recv[
                    :, jnp.where(j < HALF, i * HALF, later) + j
                ].reshape(128, 128),
            )
        else:
            apply(
                src,
                jnp.maximum(served, low),
                jnp.minimum(count, low + SLOTS),
                lambda j, entry, src=src: recv[src, :, j - low].reshape(128, 128),
            )
    if first_round:
        apply(t, 0, lists_ref[t, t, COUNT], lambda j, entry: own_v[lax.shift_right_logical(entry, 11)])

    @pl.loop(0, 8)
    def _(i):
        span = pl.ds(pl.multiple_of(i * 128, 128), 128)
        for d in range(4):
            out_ref[d, span, :128] = acc[2 * d, span, :].astype(jnp.bfloat16)
            out_ref[d, span, 128:] = acc[2 * d + 1, span, :].astype(jnp.bfloat16)


def add_delta(step, all_lists, counts, acts, delta, recv, start=None):
    rows = acts.shape[0]
    first_round = start is not None
    smem = pl.BlockSpec(memory_space=pltpu.SMEM)
    vmem = pl.BlockSpec(memory_space=pltpu.VMEM)
    kernel = functools.partial(delta_kernel, first_round)
    if not first_round:

        def kernel(*refs):
            delta_kernel(False, *refs[:6], None, *refs[6:])

    return pl.pallas_call(
        kernel,
        out_shape=(
            jax.ShapeDtypeStruct((4, rows, 256), jnp.bfloat16),
            jax.ShapeDtypeStruct((8, 128), jnp.int32),
        ),
        in_specs=[smem, smem, smem, vmem, vmem, vmem] + [vmem] * first_round,
        out_specs=(vmem, vmem),
        scratch_shapes=[
            pltpu.SMEM((16,), jnp.int32),
            pltpu.VMEM((8, rows, 128) if not first_round else (8, 8, 128), jnp.float32),
        ],
        compiler_params=pltpu.CompilerParams(vmem_limit_bytes=28 * MIB),
        name="add_delta",
    )(step, all_lists, counts, acts, delta, recv, *([start] if first_round else []))


PIECES = 4


def reduce_kernel(
    part, flag, out_ref, longest_ref,
    mine, in_a, in_b, f_a, f_b, g_a, g_b, s_a, s_b, flags, load_sem, send_sem, recv_sem, flag_s, flag_r,
):
    me = lax.axis_index("replica")
    right, left, far = (me + 1) % 4, (me + 3) % 4, (me + 2) % 4
    half = part.shape[1] // 2
    size = half // PIECES

    loads = [
        pltpu.make_async_copy(part.at[right, pl.ds(0, half)], mine.at[0], load_sem.at[0]),
        pltpu.make_async_copy(part.at[left, pl.ds(half, half)], mine.at[1], load_sem.at[1]),
        pltpu.make_async_copy(part.at[me, pl.ds(0, half)], mine.at[2], load_sem.at[2]),
        pltpu.make_async_copy(part.at[me, pl.ds(half, half)], mine.at[3], load_sem.at[3]),
    ]
    for load in loads:
        load.start()
    barrier = pltpu.get_barrier_semaphore()
    for who in (right, left, far):
        pl.semaphore_signal(barrier, inc=1, device_id={"replica": who}, device_id_type=MESH)
    pl.semaphore_wait(barrier, 3)

    started = []

    def send(kind, piece, src, dst, who):
        copy = pltpu.make_async_remote_copy(
            src_ref=src,
            dst_ref=dst,
            send_sem=send_sem.at[kind, piece],
            recv_sem=recv_sem.at[kind, piece],
            device_id={"replica": who},
            device_id_type=MESH,
        )
        copy.start()
        started.append(copy)
        return copy

    ins_a, ins_b, fs_a, fs_b, gs_a, gs_b = [], [], [], [], [], []
    for p in range(PIECES):
        span = pl.ds(p * size, size)
        low, high = pl.ds(p * size, size), pl.ds(half + p * size, size)
        ins_a.append(send(0, p, part.at[far, low], in_a.at[span], right))
        ins_b.append(send(1, p, part.at[far, high], in_b.at[span], left))
    for p in range(PIECES):
        span = pl.ds(p * size, size)
        low, high = pl.ds(p * size, size), pl.ds(half + p * size, size)
        fs_b.append(send(2, p, part.at[right, high], f_b.at[span], right))
        fs_a.append(send(3, p, part.at[left, low], f_a.at[span], left))
    told = []
    for i, who in enumerate((right, left, far)):
        copy = pltpu.make_async_remote_copy(
            src_ref=flag,
            dst_ref=flags.at[i],
            send_sem=flag_s.at[i],
            recv_sem=flag_r.at[i],
            device_id={"replica": who},
            device_id_type=MESH,
        )
        copy.start()
        told.append(copy)
    loads[0].wait()
    loads[1].wait()
    for p in range(PIECES):
        span = pl.ds(p * size, size)
        ins_a[p].wait_recv()
        s_a[span, :] = (mine[0, span, :].astype(jnp.float32) + in_a[span, :].astype(jnp.float32)).astype(jnp.bfloat16)
        gs_a.append(send(4, p, s_a.at[span], g_a.at[span], right))
        ins_b[p].wait_recv()
        s_b[span, :] = (mine[1, span, :].astype(jnp.float32) + in_b[span, :].astype(jnp.float32)).astype(jnp.bfloat16)
        gs_b.append(send(5, p, s_b.at[span], g_b.at[span], left))
    loads[2].wait()
    loads[3].wait()
    for p in range(PIECES):
        span = pl.ds(p * size, size)
        fs_a[p].wait_recv()
        gs_a[p].wait_recv()
        out_ref[pl.ds(p * size, size), :] = (
            mine[2, span, :].astype(jnp.float32) + f_a[span, :].astype(jnp.float32) + g_a[span, :].astype(jnp.float32)
        ).astype(jnp.bfloat16)
        fs_b[p].wait_recv()
        gs_b[p].wait_recv()
        out_ref[pl.ds(half + p * size, size), :] = (
            mine[3, span, :].astype(jnp.float32) + f_b[span, :].astype(jnp.float32) + g_b[span, :].astype(jnp.float32)
        ).astype(jnp.bfloat16)
    for copy in told:
        copy.wait_recv()
    longest = jnp.maximum(jnp.maximum(flags[0], flags[1]), jnp.maximum(flags[2], flag[...]))
    longest_ref[0] = jnp.max(longest)
    for copy in started + told:
        copy.wait_send()


def reduce_blocks(part, flag):
    _, rows, columns = part.shape
    half = rows // 2
    return pl.pallas_call(
        reduce_kernel,
        out_shape=(
            jax.ShapeDtypeStruct((rows, columns), jnp.bfloat16),
            jax.ShapeDtypeStruct((1,), jnp.int32),
        ),
        in_specs=[pl.BlockSpec(memory_space=pl.ANY), pl.BlockSpec(memory_space=pltpu.VMEM)],
        out_specs=(pl.BlockSpec(memory_space=pltpu.VMEM), pl.BlockSpec(memory_space=pltpu.SMEM)),
        scratch_shapes=[pltpu.VMEM((4, half, columns), jnp.bfloat16)]
        + [pltpu.VMEM((half, columns), jnp.bfloat16)] * 8
        + [pltpu.VMEM((3, 8, 128), jnp.int32)]
        + [
            pltpu.SemaphoreType.DMA((4,)),
            pltpu.SemaphoreType.DMA((6, PIECES)),
            pltpu.SemaphoreType.DMA((6, PIECES)),
            pltpu.SemaphoreType.DMA((3,)),
            pltpu.SemaphoreType.DMA((3,)),
        ],
        compiler_params=pltpu.CompilerParams(
            collective_id=2, has_side_effects=True, vmem_limit_bytes=16 * MIB
        ),
        name="reduce_blocks",
    )(part, flag)


def body(acts, base_weight, delta_blocks, block_index, tenant_counts):
    delta = delta_blocks.reshape(-1, 128, 128)
    step = jnp.zeros((1,), jnp.int32)
    lists = list_tiles(block_index)
    recv, all_lists, base, acts_v = first_exchange(lists, delta, acts, base_weight)
    part, flag = add_delta(step, all_lists, tenant_counts, acts_v, delta, recv, base)
    out, longest = reduce_blocks(part, flag)

    def another(n, out):
        step = jnp.full((1,), n - 1, jnp.int32)
        recv = exchange(step, lists, delta, base_weight)
        part, flag = add_delta(step, all_lists, tenant_counts, acts, delta, recv)
        more, _ = reduce_blocks(part, flag)
        return (out.astype(jnp.float32) + more.astype(jnp.float32)).astype(jnp.bfloat16)

    return lax.fori_loop(1, 1 + lax.div(longest[0] + (SLOTS - 1), SLOTS), another, out)


def solution(mesh):
    placed = (
        P("row", "replica"),
        P("replica", "tenant"),
        P("tenant", "replica", None, None),
        P("tenant", "replica"),
        P("row", None),
    )
    return jax.shard_map(
        body, mesh=mesh, in_specs=placed, out_specs=P("row", ("tenant", "replica")), check_vma=False
    )
```

```python
import functools

import jax
import jax.numpy as jnp
from jax import lax
from jax.experimental import pallas as pl
from jax.experimental.pallas import tpu as pltpu
from jax.sharding import PartitionSpec as P

SLOTS = 28
HALF = SLOTS // 2
SPARE = 28
GATHERED = 7 * HALF + SPARE
STARTS = (0, 2 * HALF, 4 * HALF, 6 * HALF, 7 * HALF)
SIZES = (2 * HALF, 2 * HALF, 2 * HALF, HALF, SPARE)
COUNT = 127
AHEAD = 8
OFFSETS = (1, 7, 2, 6, 3, 5, 4)
MESH = pl.DeviceIdType.MESH
MIB = 1 << 20


def list_kernel(index_ref, lists_ref):
    tenants, tiles = index_ref.shape
    counts = (jnp.int32(0), jnp.int32(0))
    for tenant in range(tenants):

        def place(n, counts):
            where = index_ref[tenant, n]
            dest = lax.shift_right_logical(where & 63, 3)
            byte = (dest & 3) * 8
            first = dest < 4
            word = jnp.where(first, counts[0], counts[1])
            count = lax.shift_right_logical(word, byte) & 255
            lists_ref[dest, count] = where + tenant * 1024 + (tenant * tiles + n) * 2048
            one = lax.shift_left(jnp.int32(1), byte)
            return counts[0] + jnp.where(first, one, 0), counts[1] + jnp.where(first, 0, one)

        counts = lax.fori_loop(0, tiles, place, counts, unroll=4)
    for dest in range(8):
        lists_ref[dest, COUNT] = lax.shift_right_logical(counts[dest // 4], (dest % 4) * 8) & 255


def list_tiles(block_index):
    return pl.pallas_call(
        list_kernel,
        out_shape=jax.ShapeDtypeStruct((8, 128), jnp.int32),
        in_specs=[pl.BlockSpec(memory_space=pltpu.SMEM)],
        out_specs=pl.BlockSpec(memory_space=pltpu.SMEM),
        compiler_params=pltpu.CompilerParams(vmem_limit_bytes=1 * MIB),
        cost_estimate=pl.CostEstimate(flops=0, bytes_accessed=8 * MIB, transcendentals=0),
        name="list_tiles",
    )(block_index)


def pick(lists_ref, slab, out_ref, dest, first):
    count = lists_ref[dest, COUNT]

    def one(s, carry):
        at = first + s
        entry = lists_ref[dest, jnp.minimum(at, COUNT)]
        tile = jnp.where(at < count, lax.shift_right_logical(entry, 11), 0)
        out_ref[s] = slab[tile]
        return carry

    lax.fori_loop(0, SLOTS, one, 0, unroll=4)


def send_to(axis):
    def remote(src, dst, s, r, who):
        return pltpu.make_async_remote_copy(
            src_ref=src, dst_ref=dst, send_sem=s, recv_sem=r, device_id={axis: who}, device_id_type=MESH
        )

    return remote


def ring():
    part = lax.axis_index("row")
    core = part % 2
    y = part // 2
    up = ((y + 1) % 4) * 2 + core
    down = ((y + 3) % 4) * 2 + core
    far = ((y + 2) % 4) * 2 + core
    twin = y * 2 + (1 - core)
    return part, up, down, far, twin


def greet(t, up, down, twin):
    barrier = pltpu.get_barrier_semaphore()
    for k in OFFSETS:
        pl.semaphore_signal(barrier, inc=1, device_id={"tenant": (t + k) % 8}, device_id_type=MESH)
    for other in (up, down, twin):
        pl.semaphore_signal(barrier, inc=1, device_id={"row": other}, device_id_type=MESH)
    pl.semaphore_wait(barrier, 10)


def first_exchange_kernel(
    lists_ref, lists, delta, acts, weight, recv, all_lists, base, acts_v,
    slab, outgoing, second, known, weight_v, load_sem,
    z_s, z_r, l_s, l_r, up_s, up_r, dn_s, dn_r, fw_s, fw_r, co_s, co_r,
):
    t = lax.axis_index("tenant")
    part, up, down, far, twin = ring()
    tenant_copy, row_copy = send_to("tenant"), send_to("row")
    loads = [
        pltpu.make_async_copy(
            delta.at[:, pl.ds(pl.multiple_of(part * 16, 16), 16), :], slab, load_sem.at[0]
        ),
        pltpu.make_async_copy(lists, all_lists.at[t], load_sem.at[1]),
        pltpu.make_async_copy(weight, weight_v, load_sem.at[2]),
        pltpu.make_async_copy(acts, acts_v, load_sem.at[3]),
    ]
    for load in loads:
        load.start()
    greet(t, up, down, twin)

    sent = []

    def go(copy):
        copy.start()
        sent.append(copy)
        return copy

    tables = []
    for i, k in enumerate(OFFSETS):
        tables.append(go(tenant_copy(lists, all_lists.at[t], l_s.at[i], l_r.at[i], (t + k) % 8)))
    loads[0].wait()
    z_copies = []
    for i, k in enumerate(OFFSETS):
        dest = (t + k) % 8
        pick(lists_ref, slab, outgoing.at[i], dest, 0)
        copy = tenant_copy(
            outgoing.at[i, pl.ds(0, HALF)], recv.at[part, pl.ds(i * HALF, HALF)], z_s.at[i], z_r.at[i], dest
        )
        if i < AHEAD:
            go(copy)
        z_copies.append(copy)
    for i, k in enumerate(OFFSETS):
        copy = tenant_copy(
            outgoing.at[i, pl.ds(HALF, HALF)], second.at[i], z_s.at[7 + i], z_r.at[7 + i], (t + k) % 8
        )
        if 7 + i < AHEAD:
            go(copy)
        z_copies.append(copy)
    loads[1].wait()
    for table in tables:
        table.wait_recv()
    learn = pltpu.make_async_copy(all_lists, known, load_sem.at[4])
    learn.start()
    learn.wait()

    ups, downs, forwards, twins = {}, {}, {}, []

    def spans(g):
        half = SIZES[g] // 2
        return pl.ds(STARTS[g], half), pl.ds(STARTS[g] + half, half)

    def share(g, n, owner):
        block = recv.at[owner, pl.ds(STARTS[g], SIZES[g])]
        twins.append(go(row_copy(block, block, co_s.at[g, n], co_r.at[g, n], twin)))

    def landed(i):
        z_copies[i].wait_recv()
        if i + AHEAD < 14:
            go(z_copies[i + AHEAD])

    def compact():
        ends = []
        total = jnp.int32(0)
        for k in OFFSETS:
            total = total + jnp.clip(known[(t + 8 - k) % 8, t, COUNT] - HALF, 0, HALF)
            ends.append(total)

        def one(s, carry):
            src, begin = jnp.int32(0), jnp.int32(0)
            for end in ends:
                past = s >= end
                src = src + jnp.where(past, 1, 0)
                begin = jnp.where(past, end, begin)
            recv[part, STARTS[4] + s] = second[jnp.minimum(src, 6), jnp.clip(s - begin, 0, HALF - 1)]
            return carry

        lax.fori_loop(0, SPARE, one, 0, unroll=2)

    def spread(g):
        low, high = spans(g)
        a, b = recv.at[part, low], recv.at[part, high]
        ups[g, 0] = go(row_copy(a, a, up_s.at[g, 0], up_r.at[g, 0], up))
        downs[g, 1] = go(row_copy(b, b, dn_s.at[g, 1], dn_r.at[g, 1], down))
        ups[g, 1] = go(row_copy(b, b, up_s.at[g, 1], up_r.at[g, 1], up))
        downs[g, 0] = go(row_copy(a, a, dn_s.at[g, 0], dn_r.at[g, 0], down))
        share(g, 0, part)

    def neighbours(g):
        low, high = spans(g)
        ups[g, 0].wait_recv()
        a = recv.at[down, low]
        forwards[g, 0] = go(row_copy(a, a, fw_s.at[g, 0], fw_r.at[g, 0], up))
        downs[g, 1].wait_recv()
        b = recv.at[up, high]
        forwards[g, 1] = go(row_copy(b, b, fw_s.at[g, 1], fw_r.at[g, 1], down))
        ups[g, 1].wait_recv()
        share(g, 1, down)
        downs[g, 0].wait_recv()
        share(g, 2, up)

    def opposite(g):
        forwards[g, 0].wait_recv()
        forwards[g, 1].wait_recv()
        share(g, 3, far)

    def multiply(i):
        if i == 0:
            loads[2].wait()
            loads[3].wait()
        rows = pl.ds(i * 256, 256)

        @pl.loop(0, 2)
        def _(c):
            out = jnp.dot(
                acts_v[rows, :],
                weight_v[:, pl.ds(pl.multiple_of(c * 512, 512), 512)],
                preferred_element_type=jnp.float32,
            )
            for n in range(4):
                base[4 * c + n, rows, :] = out[:, n * 128 : (n + 1) * 128]

    def arrived(g):
        for i in (2 * g, 2 * g + 1) if g < 3 else (6,):
            landed(i)
        spread(g)

    arrived(0)
    multiply(0)
    arrived(1)
    neighbours(0)
    multiply(1)
    arrived(2)
    opposite(0)
    neighbours(1)
    multiply(2)
    arrived(3)
    neighbours(2)
    opposite(1)
    landed(7)
    landed(8)
    multiply(3)
    neighbours(3)
    opposite(2)
    landed(9)
    landed(10)
    opposite(3)
    landed(11)
    landed(12)
    landed(13)
    compact()
    spread(4)
    neighbours(4)
    opposite(4)
    for copy in twins:
        copy.wait_recv()
    for copy in sent:
        copy.wait_send()


def first_exchange(lists, delta, acts, weight):
    rows, depth = acts.shape
    columns = weight.shape[1]
    any_spec = pl.BlockSpec(memory_space=pl.ANY)
    vmem = pl.BlockSpec(memory_space=pltpu.VMEM)
    dma = pltpu.SemaphoreType.DMA
    return pl.pallas_call(
        first_exchange_kernel,
        out_shape=(
            jax.ShapeDtypeStruct((8, GATHERED, 16, 128), jnp.bfloat16),
            jax.ShapeDtypeStruct((8, 8, 128), jnp.int32),
            jax.ShapeDtypeStruct((columns // 128, rows, 128), jnp.float32),
            jax.ShapeDtypeStruct((rows, depth), jnp.bfloat16),
        ),
        in_specs=[
            pl.BlockSpec(memory_space=pltpu.SMEM),
            any_spec,
            any_spec,
            pl.BlockSpec(memory_space=pltpu.HBM),
            pl.BlockSpec(memory_space=pltpu.HBM),
        ],
        out_specs=(vmem, any_spec, vmem, vmem),
        scratch_shapes=[
            pltpu.VMEM((delta.shape[0], 16, 128), jnp.bfloat16),
            pltpu.VMEM((7, SLOTS, 16, 128), jnp.bfloat16),
        ]
        + [
            pltpu.VMEM((7, HALF, 16, 128), jnp.bfloat16),
            pltpu.SMEM((8, 8, 128), jnp.int32),
            pltpu.VMEM((depth, columns), jnp.bfloat16),
            dma((5,)),
        ]
        + [dma((14,))] * 2
        + [dma((7,))] * 2
        + [dma((5, 2))] * 6
        + [dma((5, 4))] * 2,
        compiler_params=pltpu.CompilerParams(
            collective_id=0, has_side_effects=True, vmem_limit_bytes=28 * MIB
        ),
        name="exchange_tiles_base",
    )(lists, lists, delta, acts, weight)


def exchange_kernel(
    round_ref, lists_ref, delta, unused_weight, recv, slab, outgoing, load_sem,
    z_s, z_r, up_s, up_r, dn_s, dn_r, fw_s, fw_r, co_s, co_r,
):
    t = lax.axis_index("tenant")
    part, up, down, far, twin = ring()
    tenant_copy, row_copy = send_to("tenant"), send_to("row")
    load = pltpu.make_async_copy(
        delta.at[:, pl.ds(pl.multiple_of(part * 16, 16), 16), :], slab, load_sem
    )
    load.start()
    greet(t, up, down, twin)
    load.wait()
    half = SLOTS // 2
    low, high = pl.ds(0, half), pl.ds(half, half)
    for i, k in enumerate(OFFSETS):
        dest = (t + k) % 8
        src = (t + 8 - k) % 8
        pick(lists_ref, slab, outgoing.at[i], dest, round_ref[0] * SLOTS)
        copies = [tenant_copy(outgoing.at[i], recv.at[t, part], z_s.at[i], z_r.at[i], dest)]
        copies[0].start()
        copies[0].wait_recv()

        def go(block, s, r, who):
            copy = row_copy(block, block, s, r, who)
            copy.start()
            copies.append(copy)
            return copy

        block = recv.at[src, part]
        raised = go(block, up_s.at[i], up_r.at[i], up)
        lowered = go(block, dn_s.at[i], dn_r.at[i], down)
        twins = [go(block, co_s.at[i, 0], co_r.at[i, 0], twin)]
        raised.wait_recv()
        lowered.wait_recv()
        one = go(recv.at[src, down, low], fw_s.at[i, 0], fw_r.at[i, 0], up)
        two = go(recv.at[src, up, high], fw_s.at[i, 1], fw_r.at[i, 1], down)
        twins.append(go(recv.at[src, down], co_s.at[i, 1], co_r.at[i, 1], twin))
        twins.append(go(recv.at[src, up], co_s.at[i, 2], co_r.at[i, 2], twin))
        one.wait_recv()
        two.wait_recv()
        twins.append(go(recv.at[src, far], co_s.at[i, 3], co_r.at[i, 3], twin))
        for copy in twins:
            copy.wait_recv()
        for copy in copies:
            copy.wait_send()


def exchange(step, lists, delta, weight):
    dma = pltpu.SemaphoreType.DMA
    return pl.pallas_call(
        exchange_kernel,
        out_shape=jax.ShapeDtypeStruct((8, 8, SLOTS, 16, 128), jnp.bfloat16),
        in_specs=[pl.BlockSpec(memory_space=pltpu.SMEM)] * 2 + [pl.BlockSpec(memory_space=pl.ANY)] * 2,
        out_specs=pl.BlockSpec(memory_space=pltpu.VMEM),
        scratch_shapes=[
            pltpu.VMEM((delta.shape[0], 16, 128), jnp.bfloat16),
            pltpu.VMEM((7, SLOTS, 16, 128), jnp.bfloat16),
            dma,
        ]
        + [dma((7,))] * 6
        + [dma((7, 2))] * 2
        + [dma((7, 4))] * 2,
        compiler_params=pltpu.CompilerParams(
            collective_id=1, has_side_effects=True, vmem_limit_bytes=16 * MIB
        ),
        name="exchange_tiles",
    )(step, lists, delta, weight)


GROUP = 8
CHUNK = 128


def delta_kernel(
    first_round, round_ref, lists_ref, counts_ref, acts_v, own_v, recv, start_ref, out_ref, flag_ref,
    offsets, acc,
):
    t = lax.axis_index("tenant")
    low = round_ref[0] * SLOTS
    rows = acts_v.shape[0]
    longest, over = jnp.int32(0), jnp.int32(0)
    for dest in range(8):
        spare = jnp.int32(0)
        for k in range(1, 8):
            length = lists_ref[(dest + k) % 8, dest, COUNT]
            longest = jnp.maximum(longest, length)
            spare = spare + jnp.maximum(length - HALF, 0)
        over = jnp.maximum(over, spare - SPARE)
    over = jnp.maximum(over, longest - SLOTS)
    flag_ref[...] = jnp.full(flag_ref.shape, jnp.where(over > 0, longest, 0), jnp.int32)
    total = jnp.int32(0)
    for tenant in range(16):
        offsets[tenant] = total
        total = total + counts_ref[0, tenant]
    if first_round:
        acc = start_ref
    else:
        acc[...] = jnp.zeros_like(acc)

    line = lax.broadcasted_iota(jnp.int32, (CHUNK, 128), 0)

    def apply(src, begin, end, tile_of):
        def group(g, carry):
            work = []
            chunks = jnp.int32(0)
            for u in range(GROUP):
                j = begin + g * GROUP + u
                valid = j < end
                j = jnp.minimum(j, end - 1)
                entry = lists_ref[src, t, j]
                tenant = 2 * src + (lax.shift_right_logical(entry, 10) & 1)
                brow = lax.shift_right_logical(entry, 6) & 15
                bcol = entry & 7
                lo = offsets[tenant]
                hi = jnp.where(valid, lo + counts_ref[0, tenant], 0)
                base = lax.shift_right_logical(lo, 4) * 16
                chunks = jnp.maximum(chunks, lax.shift_right_arithmetic(hi - base + CHUNK - 1, 7))
                work.append((j, entry, brow, bcol, lo, hi, base))

            def chunk(i, carry):
                products = []
                for j, entry, brow, bcol, lo, hi, base in work:
                    at = pl.multiple_of(jnp.minimum(base + i * CHUNK, rows - CHUNK), 16)
                    x = acts_v[pl.ds(at, CHUNK), pl.ds(pl.multiple_of(brow * 128, 128), 128)]
                    out = jnp.dot(x, tile_of(j, entry), preferred_element_type=jnp.float32)
                    products.append((at, jnp.maximum(lo, base + i * CHUNK), hi, bcol, out))
                for at, lo, hi, bcol, out in products:
                    keep = (line >= lo - at) & (line < hi - at)
                    acc[bcol, pl.ds(at, CHUNK), :] += jnp.where(keep, out, 0.0)
                return carry

            lax.fori_loop(0, chunks, chunk, 0)
            return carry

        lax.fori_loop(0, lax.div(jnp.maximum(end - begin, 0) + GROUP - 1, GROUP), group, 0)

    begin = jnp.int32(0)
    for i, k in enumerate(OFFSETS):
        src = (t + 8 - k) % 8
        count = lists_ref[src, t, COUNT]
        served = jnp.minimum(count, HALF + jnp.clip(SPARE - begin, 0, HALF))
        later = 7 * HALF + begin - HALF
        begin = begin + jnp.clip(count - HALF, 0, HALF)
        if first_round:
            apply(
                src,
                0,
                served,
                lambda j, entry, i=i, later=later: recv[
                    :, jnp.where(j < HALF, i * HALF, later) + j
                ].reshape(128, 128),
            )
        else:
            apply(
                src,
                jnp.maximum(served, low),
                jnp.minimum(count, low + SLOTS),
                lambda j, entry, src=src: recv[src, :, j - low].reshape(128, 128),
            )
    if first_round:
        apply(t, 0, lists_ref[t, t, COUNT], lambda j, entry: own_v[lax.shift_right_logical(entry, 11)])

    @pl.loop(0, 8)
    def _(i):
        span = pl.ds(pl.multiple_of(i * 128, 128), 128)
        for d in range(4):
            out_ref[d, span, :128] = acc[2 * d, span, :].astype(jnp.bfloat16)
            out_ref[d, span, 128:] = acc[2 * d + 1, span, :].astype(jnp.bfloat16)


def add_delta(step, all_lists, counts, acts, delta, recv, start=None):
    rows = acts.shape[0]
    first_round = start is not None
    smem = pl.BlockSpec(memory_space=pltpu.SMEM)
    vmem = pl.BlockSpec(memory_space=pltpu.VMEM)
    kernel = functools.partial(delta_kernel, first_round)
    if not first_round:

        def kernel(*refs):
            delta_kernel(False, *refs[:6], None, *refs[6:])

    return pl.pallas_call(
        kernel,
        out_shape=(
            jax.ShapeDtypeStruct((4, rows, 256), jnp.bfloat16),
            jax.ShapeDtypeStruct((8, 128), jnp.int32),
        ),
        in_specs=[smem, smem, smem, vmem, vmem, vmem] + [vmem] * first_round,
        out_specs=(vmem, vmem),
        scratch_shapes=[
            pltpu.SMEM((16,), jnp.int32),
            pltpu.VMEM((8, rows, 128) if not first_round else (8, 8, 128), jnp.float32),
        ],
        compiler_params=pltpu.CompilerParams(vmem_limit_bytes=28 * MIB),
        name="add_delta",
    )(step, all_lists, counts, acts, delta, recv, *([start] if first_round else []))


PIECES = 4


def reduce_kernel(
    part, flag, out_ref, longest_ref,
    mine, in_a, in_b, f_a, f_b, g_a, g_b, s_a, s_b, flags, load_sem, send_sem, recv_sem, flag_s, flag_r,
):
    me = lax.axis_index("replica")
    right, left, far = (me + 1) % 4, (me + 3) % 4, (me + 2) % 4
    half = part.shape[1] // 2
    size = half // PIECES

    loads = [
        pltpu.make_async_copy(part.at[right, pl.ds(0, half)], mine.at[0], load_sem.at[0]),
        pltpu.make_async_copy(part.at[left, pl.ds(half, half)], mine.at[1], load_sem.at[1]),
        pltpu.make_async_copy(part.at[me, pl.ds(0, half)], mine.at[2], load_sem.at[2]),
        pltpu.make_async_copy(part.at[me, pl.ds(half, half)], mine.at[3], load_sem.at[3]),
    ]
    for load in loads:
        load.start()
    barrier = pltpu.get_barrier_semaphore()
    for who in (right, left, far):
        pl.semaphore_signal(barrier, inc=1, device_id={"replica": who}, device_id_type=MESH)
    pl.semaphore_wait(barrier, 3)

    started = []

    def send(kind, piece, src, dst, who):
        copy = pltpu.make_async_remote_copy(
            src_ref=src,
            dst_ref=dst,
            send_sem=send_sem.at[kind, piece],
            recv_sem=recv_sem.at[kind, piece],
            device_id={"replica": who},
            device_id_type=MESH,
        )
        copy.start()
        started.append(copy)
        return copy

    ins_a, ins_b, fs_a, fs_b, gs_a, gs_b = [], [], [], [], [], []
    for p in range(PIECES):
        span = pl.ds(p * size, size)
        low, high = pl.ds(p * size, size), pl.ds(half + p * size, size)
        ins_a.append(send(0, p, part.at[far, low], in_a.at[span], right))
        ins_b.append(send(1, p, part.at[far, high], in_b.at[span], left))
    for p in range(PIECES):
        span = pl.ds(p * size, size)
        low, high = pl.ds(p * size, size), pl.ds(half + p * size, size)
        fs_b.append(send(2, p, part.at[right, high], f_b.at[span], right))
        fs_a.append(send(3, p, part.at[left, low], f_a.at[span], left))
    told = []
    for i, who in enumerate((right, left, far)):
        copy = pltpu.make_async_remote_copy(
            src_ref=flag,
            dst_ref=flags.at[i],
            send_sem=flag_s.at[i],
            recv_sem=flag_r.at[i],
            device_id={"replica": who},
            device_id_type=MESH,
        )
        copy.start()
        told.append(copy)
    loads[0].wait()
    loads[1].wait()
    for p in range(PIECES):
        span = pl.ds(p * size, size)
        ins_a[p].wait_recv()
        s_a[span, :] = (mine[0, span, :].astype(jnp.float32) + in_a[span, :].astype(jnp.float32)).astype(jnp.bfloat16)
        gs_a.append(send(4, p, s_a.at[span], g_a.at[span], right))
        ins_b[p].wait_recv()
        s_b[span, :] = (mine[1, span, :].astype(jnp.float32) + in_b[span, :].astype(jnp.float32)).astype(jnp.bfloat16)
        gs_b.append(send(5, p, s_b.at[span], g_b.at[span], left))
    loads[2].wait()
    loads[3].wait()
    for p in range(PIECES):
        span = pl.ds(p * size, size)
        fs_a[p].wait_recv()
        gs_a[p].wait_recv()
        out_ref[pl.ds(p * size, size), :] = (
            mine[2, span, :].astype(jnp.float32) + f_a[span, :].astype(jnp.float32) + g_a[span, :].astype(jnp.float32)
        ).astype(jnp.bfloat16)
        fs_b[p].wait_recv()
        gs_b[p].wait_recv()
        out_ref[pl.ds(half + p * size, size), :] = (
            mine[3, span, :].astype(jnp.float32) + f_b[span, :].astype(jnp.float32) + g_b[span, :].astype(jnp.float32)
        ).astype(jnp.bfloat16)
    for copy in told:
        copy.wait_recv()
    longest = jnp.maximum(jnp.maximum(flags[0], flags[1]), jnp.maximum(flags[2], flag[...]))
    longest_ref[0] = jnp.max(longest)
    for copy in started + told:
        copy.wait_send()


def reduce_blocks(part, flag):
    _, rows, columns = part.shape
    half = rows // 2
    return pl.pallas_call(
        reduce_kernel,
        out_shape=(
            jax.ShapeDtypeStruct((rows, columns), jnp.bfloat16),
            jax.ShapeDtypeStruct((1,), jnp.int32),
        ),
        in_specs=[pl.BlockSpec(memory_space=pl.ANY), pl.BlockSpec(memory_space=pltpu.VMEM)],
        out_specs=(pl.BlockSpec(memory_space=pltpu.VMEM), pl.BlockSpec(memory_space=pltpu.SMEM)),
        scratch_shapes=[pltpu.VMEM((4, half, columns), jnp.bfloat16)]
        + [pltpu.VMEM((half, columns), jnp.bfloat16)] * 8
        + [pltpu.VMEM((3, 8, 128), jnp.int32)]
        + [
            pltpu.SemaphoreType.DMA((4,)),
            pltpu.SemaphoreType.DMA((6, PIECES)),
            pltpu.SemaphoreType.DMA((6, PIECES)),
            pltpu.SemaphoreType.DMA((3,)),
            pltpu.SemaphoreType.DMA((3,)),
        ],
        compiler_params=pltpu.CompilerParams(
            collective_id=2, has_side_effects=True, vmem_limit_bytes=16 * MIB
        ),
        name="reduce_blocks",
    )(part, flag)


def body(acts, base_weight, delta_blocks, block_index, tenant_counts):
    delta = delta_blocks.reshape(-1, 128, 128)
    step = jnp.zeros((1,), jnp.int32)
    lists = list_tiles(block_index)
    recv, all_lists, base, acts_v = first_exchange(lists, delta, acts, base_weight)
    part, flag = add_delta(step, all_lists, tenant_counts, acts_v, delta, recv, base)
    out, longest = reduce_blocks(part, flag)

    def another(n, out):
        step = jnp.full((1,), n - 1, jnp.int32)
        recv = exchange(step, lists, delta, base_weight)
        part, flag = add_delta(step, all_lists, tenant_counts, acts, delta, recv)
        more, _ = reduce_blocks(part, flag)
        return (out.astype(jnp.float32) + more.astype(jnp.float32)).astype(jnp.bfloat16)

    return lax.fori_loop(1, 1 + lax.div(longest[0] + (SLOTS - 1), SLOTS), another, out)


def solution(mesh):
    placed = (
        P("row", "replica"),
        P("replica", "tenant"),
        P("tenant", "replica", None, None),
        P("tenant", "replica"),
        P("row", None),
    )
    return jax.shard_map(
        body, mesh=mesh, in_specs=placed, out_specs=P("row", ("tenant", "replica")), check_vma=False
    )
```
